32 devices in a mesh: space: 16 (over z, y, core), band: 2 (over x).
Axes of the slice: x: 2, y: 2, z: 4, core: 2. Of those that a mesh axis runs over, the one named last changes fastest.
Arguments:
- orbitals: float32 [320, 64, 512], P('band', 'space'), may hold values from -6 to 6
- potential: float32 [64, 512], P('space'), may hold values from -2 to 0
- rotation: float32 [320, 320], replicated, may hold values from -0.3125 to 0.3125
Outputs:
- rotated: float32 [320, 64, 512], P('band', 'space')
The draws below stay inside these ranges and needn't reach their ends.
All inputs are finite; a program needn't handle non-finite values.
Results may differ from the reference program's by a relative error of at most 0.00007.
Values sent between devices are 32-bit elements; how exact they have to be, the bound alone decides.
A program may use at most 128 MiB of HBM per device.

```python
import jax
import jax.numpy as jnp
from jax import lax

NORB = 320
DEG = 4
NY = 16
NZ = 32
PLANE = 512
NX = 64


def block_levels(stream_key, extent, split, least, largest):
    level, own = 1.0, jax.random.fold_in(stream_key, 6)
    for axis_at, blocks in split:
        draws = jnp.exp(jax.random.uniform(jax.random.fold_in(own, axis_at), (blocks,), jnp.float32, least / len(split), largest / len(split)))
        level = level * jnp.repeat(draws, extent[axis_at] // blocks).reshape([-1 if axis == axis_at else 1 for axis in range(len(extent))])
    return level


def scatter_about(key, extent, width, reach, shards=(), held_as=jnp.bfloat16):
    entries = width * jax.random.normal(key, extent, jnp.float32)
    if shards:
        entries = entries * block_levels(key, extent, shards, -0.22, 0.18)
    return jnp.clip(entries, -reach, reach).astype(held_as)


def setup_inputs(seed: int = 0) -> dict:
    arg_keys = jax.random.split(jax.random.key(seed), 4)
    return {
        "orbitals": scatter_about(arg_keys[0], (NORB, NX, PLANE), 1.0, 6.0, ((0, 2), (1, 16)), jnp.float32),
        "potential": jnp.clip(-2.0 + 2.0 * jax.random.uniform(arg_keys[1], (NX, PLANE), jnp.float32) ** block_levels(arg_keys[1], (NX, PLANE), ((0, 16),), -0.2, 0.2), -2.0, 0.0),
        "rotation": scatter_about(arg_keys[2], (NORB, NORB), NORB ** -0.5, 0.3125, (), jnp.float32),
    }


coef_lap = (-205.0 / 72.0, 8.0 / 5.0, -1.0 / 5.0, 8.0 / 315.0, -1.0 / 560.0)
center_val = 6.0
half_width = 4.0


def hamil(field, pot_grid):
    lap = (3.0 * coef_lap[0]) * field
    for shift_k in range(1, 5):
        for axis_num in (1, 2, 3):
            lap = lap + coef_lap[shift_k] * (jnp.roll(field, shift_k, axis_num) + jnp.roll(field, -shift_k, axis_num))
    return -0.5 * lap + pot_grid[None] * field


def filter_block(block, pot_grid):
    prev_y = block
    curr_y = (hamil(block, pot_grid) - center_val * block) / half_width
    for step in range(1, DEG):
        next_y = 2.0 * (hamil(curr_y, pot_grid) - center_val * curr_y) / half_width - prev_y
        prev_y = curr_y
        curr_y = next_y
    return curr_y


def reference(orbitals, potential, rotation):
    pot_grid = potential.reshape(NX, NY, NZ)
    blocks = orbitals.reshape(NORB // 16, 16, NX, NY, NZ)
    filtered = lax.map(lambda blk: filter_block(blk, pot_grid), blocks)
    filtered = filtered.reshape(NORB, NX * PLANE)
    rotated = lax.dot_general(rotation, filtered, (((0,), (0,)), ((), ())), precision=lax.Precision.HIGHEST, preferred_element_type=jnp.float32)
    return rotated.reshape(NORB, NX, PLANE)
```

```python
import functools

import jax
import jax.numpy as jnp
import numpy as np
from jax import lax
from jax.experimental import pallas as pl
from jax.experimental.pallas import tpu as pltpu
from jax.sharding import PartitionSpec as P

DEG = 4
NY = 16
NZ = 32
MESH = pl.DeviceIdType.MESH


coef_lap = (-205.0 / 72.0, 8.0 / 5.0, -1.0 / 5.0, 8.0 / 315.0, -1.0 / 560.0)
center_val = 6.0
half_width = 4.0

MAIN = 8
REST = 2
SLAB = 4
CELLS = NY * NZ
WEIGHT = [-0.5 * c / half_width for c in coef_lap]
SHIFT = -1.5 * coef_lap[0] - center_val


def with_halo(block, sides, width):
    for axis, dim in sides:
        count = lax.axis_size(axis)
        forward = [(i, i + 1) for i in range(count - 1)]
        forward.append((count - 1, 0))
        backward = [(target, source) for source, target in forward]
        low = lax.ppermute(
            lax.slice_in_dim(block, block.shape[dim] - width, None, axis=dim), axis, forward
        )
        high = lax.ppermute(lax.slice_in_dim(block, 0, width, axis=dim), axis, backward)
        block = jnp.concatenate([low, block, high], axis=dim)
    return block


def cross_terms(field):
    nblk, planes, cells = field.shape
    cube = field.reshape(nblk, planes, NY, NZ)
    inner = jnp.zeros_like(cube)
    for shift_k in range(1, 5):
        inner = inner + coef_lap[shift_k] * (
            jnp.roll(cube, shift_k, 2)
            + jnp.roll(cube, -shift_k, 2)
            + jnp.roll(cube, shift_k, 3)
            + jnp.roll(cube, -shift_k, 3)
        )
    return inner.reshape(nblk, planes, cells)


def hamil_slab(field, potential):
    planes = field.shape[1]
    padded = with_halo(field, (("space", 1),), 4)
    lap = 3.0 * coef_lap[0] * field
    for shift_k in range(1, 5):
        upper = padded[:, 4 + shift_k : 4 + shift_k + planes]
        lower = padded[:, 4 - shift_k : 4 - shift_k + planes]
        lap = lap + coef_lap[shift_k] * (upper + lower)
    lap = lap + cross_terms(field)
    return -0.5 * lap + potential[None] * field


def chebyshev(start_y, potential, apply_h):
    prev_y = start_y
    curr_y = (apply_h(start_y, potential) - center_val * start_y) / half_width
    for step in range(1, DEG):
        next_y = 2.0 * (apply_h(curr_y, potential) - center_val * curr_y) / half_width - prev_y
        prev_y = curr_y
        curr_y = next_y
    return curr_y


def local_halo(orbitals, potential, rotation):
    curr_y = chebyshev(orbitals, potential, hamil_slab)
    turned = lax.dot_general(
        rotation,
        lax.all_to_all(curr_y, "band", split_axis=2, concat_axis=0, tiled=True),
        (((0,), (0,)), ((), ())),
        precision=lax.Precision.HIGHEST,
        preferred_element_type=jnp.float32,
    )
    return lax.all_to_all(turned, "band", split_axis=0, concat_axis=2, tiled=True)


def split_const(matrix):
    high = matrix.astype(np.float32).astype(jnp.bfloat16)
    low = (matrix - high.astype(np.float64)).astype(np.float32).astype(jnp.bfloat16)
    return np.stack([high, low])


def ring_matrix(size):
    ring = np.zeros((size, size))
    for at in range(size):
        for k in range(1, 5):
            ring[at, (at + k) % size] += WEIGHT[k]
            ring[at, (at - k) % size] += WEIGHT[k]
    return ring


def in_plane():
    return split_const(
        np.kron(ring_matrix(NY), np.eye(NZ)) + np.kron(np.eye(NY), ring_matrix(NZ))
    )


def across_planes(planes):
    return split_const(np.kron(ring_matrix(planes), np.eye(REST)))


def spread(planes):
    rows = np.concatenate(
        [np.repeat(np.arange(planes), MAIN), np.repeat(np.arange(planes), REST)]
    )
    picks = np.arange(2 * planes)
    return np.stack([rows[:, None] * 2 + half == picks[None] for half in range(2)]).astype(
        jnp.bfloat16
    )


def split2(value):
    high = value.astype(jnp.bfloat16)
    low = (value - high.astype(jnp.float32)).astype(jnp.bfloat16)
    return high, low


def dot(a, b):
    return jnp.dot(a, b, preferred_element_type=jnp.float32)


def kernel(
    n,
    y_ref,
    rt_ref,
    pot_ref,
    plane_hbm,
    cross_ref,
    spread_ref,
    out_ref,
    other,
    turned,
    buf0,
    buf1,
    buf2,
    rest_send,
    rest_in,
    rest_out,
    rest_back,
    pots,
    diag,
    plane,
    acc,
    high,
    low,
    x_send,
    x_recv,
    pot_send,
    pot_recv,
    a_send,
    a_recv,
    b_send,
    b_recv,
    oa_send,
    oa_recv,
    ob_send,
    ob_recv,
    plane_sem,
):
    me = lax.axis_index("space")
    band = lax.axis_index("band")
    nx = SLAB * n
    rows = nx * MAIN
    first_rest = MAIN * n

    barrier = pltpu.get_barrier_semaphore()
    pl.semaphore_signal(
        barrier, inc=1, device_id={"band": 1 - band}, device_id_type=MESH
    )

    def peers(body):
        def step(k, carry):
            body(lax.rem(me + k, n))
            return carry

        lax.fori_loop(1, n, step, 0)

    peers(
        lambda d: pl.semaphore_signal(
            barrier, inc=1, device_id={"space": d}, device_id_type=MESH
        )
    )
    plane_copy = pltpu.make_async_copy(plane_hbm, plane, plane_sem)
    plane_copy.start()
    pl.semaphore_wait(barrier, n)

    def x_copy(p):
        return pltpu.make_async_remote_copy(
            src_ref=y_ref.at[p],
            dst_ref=other.at[p],
            send_sem=x_send.at[p],
            recv_sem=x_recv.at[p],
            device_id={"band": 1 - band},
            device_id_type=MESH,
        )

    def space_copy(src, dst, send_sem, recv_sem, target):
        return pltpu.make_async_remote_copy(
            src_ref=src,
            dst_ref=dst,
            send_sem=send_sem,
            recv_sem=recv_sem,
            device_id={"space": target},
            device_id_type=MESH,
        )

    def main_rows(d):
        return pl.ds(pl.multiple_of(MAIN * d, MAIN), MAIN)

    def pot_copy(d, at):
        return space_copy(pot_ref, pots.at[at], pot_send.at[d], pot_recv.at[at], d)

    def a_plane(d, at, p):
        return space_copy(
            turned.at[p, main_rows(d), :],
            buf0.at[4 + SLAB * at + p],
            a_send.at[d],
            a_recv.at[at],
            d,
        )

    def a_whole(d, at):
        return space_copy(
            turned.at[:, main_rows(d), :],
            buf0.at[pl.ds(4 + SLAB * at, SLAB)],
            a_send.at[d],
            a_recv.at[at],
            d,
        )

    def b_copy(d, at):
        return space_copy(rest_send.at[d], rest_in.at[at], b_send.at[d], b_recv.at[at], d)

    def oa_copy(d, at):
        return space_copy(
            buf1.at[pl.ds(4 + SLAB * d, SLAB)],
            out_ref.at[:, main_rows(at), :],
            oa_send.at[d],
            oa_recv.at[at],
            d,
        )

    def ob_copy(d, at):
        return space_copy(rest_out.at[d], rest_back.at[at], ob_send.at[d], ob_recv.at[at], d)

    for p in range(SLAB):
        x_copy(p).start()
    peers(lambda d: pot_copy(d, me).start())
    pots[me] = pot_ref[...]

    own_high, own_low = split2(rt_ref[0])
    oth_high, oth_low = split2(rt_ref[1])
    for p in range(SLAB):
        vh, vl = split2(y_ref[p])
        turned[p] = dot(own_high, vh) + dot(own_high, vl) + dot(own_low, vh)
    for p in range(SLAB):
        x_copy(p).wait_recv()
        vh, vl = split2(other[p])
        turned[p] += dot(oth_high, vh) + dot(oth_high, vl) + dot(oth_low, vh)
        peers(lambda d, p=p: a_plane(d, me, p).start())
        buf0[4 + SLAB * me + p] = turned[p, main_rows(me), :]
        for d in range(n):
            rest_send[d, REST * p : REST * p + REST, :] = turned[
                p, first_rest + REST * d : first_rest + REST * d + REST, :
            ]
    peers(lambda d: b_copy(d, me).start())
    rest_in[me] = rest_send[me]

    peers(lambda s: pot_copy(s, s).wait_recv())
    field = pots[...].reshape(2 * nx, CELLS // 2)
    fh, rem = field.astype(jnp.bfloat16), field
    rem = rem - fh.astype(jnp.float32)
    fm, fl = split2(rem)
    for half in range(2):
        pick = spread_ref[half]
        diag[:, half * (CELLS // 2) : (half + 1) * (CELLS // 2)] = (
            dot(pick, fh) + dot(pick, fm) + dot(pick, fl) + SHIFT
        ) * (1.0 / half_width)

    plane_copy.wait()

    def wrap(ref):
        ref[0:4] = ref[nx : nx + 4]
        ref[nx + 4 : nx + 8] = ref[4:8]

    def put_split(g, lanes, value):
        flat = value.reshape(8 * MAIN, 128)
        hi, lo = split2(flat)
        at = pl.ds(pl.multiple_of(g * (8 * MAIN), 8 * MAIN), 8 * MAIN)
        high[at, lanes] = hi
        low[at, lanes] = lo

    def each_group(body):
        def step(g, carry):
            for c in range(CELLS // 128):
                body(g, slice(128 * c, 128 * c + 128))
            return carry

        lax.fori_loop(0, nx // 8, step, 0)

    peers(lambda s: a_whole(s, s).wait_recv())
    wrap(buf0)
    each_group(
        lambda g, lanes: put_split(g, lanes, buf0[pl.ds(g * 8 + 4, 8), :, lanes])
    )
    block = min(rows, 256)
    order = [(buf0, None, buf1), (buf1, buf0, buf2), (buf2, buf1, buf0), (buf0, buf2, buf1)]
    for number, (cur, prev, new) in enumerate(order):
        last = number == DEG - 1
        for r in range(rows // block):
            at = slice(r * block, (r + 1) * block)
            acc[at, :] = (
                dot(high[at, :], plane[0]) + dot(low[at, :], plane[0]) + dot(high[at, :], plane[1])
            )

        def update(g, lanes, cur=cur, prev=prev, new=new, last=last):
            wide = cur[pl.ds(g * 8, 16), :, lanes]
            at = pl.ds(pl.multiple_of(g * (8 * MAIN), 8 * MAIN), 8 * MAIN)
            total = acc[at, lanes].reshape(8, MAIN, 128)
            total = total + diag[at, lanes].reshape(8, MAIN, 128) * wide[4:12]
            for k in range(1, 5):
                total = total + WEIGHT[k] * (wide[4 + k : 12 + k] + wide[4 - k : 12 - k])
            if prev is not None:
                total = 2.0 * total - prev[pl.ds(g * 8 + 4, 8), :, lanes]
            new[pl.ds(g * 8 + 4, 8), :, lanes] = total
            if not last:
                put_split(g, lanes, total)

        each_group(update)
        if not last:
            wrap(new)
    peers(lambda d: oa_copy(d, me).start())
    out_ref[:, main_rows(me), :] = buf1[pl.ds(4 + SLAB * me, SLAB)]

    peers(lambda s: b_copy(s, s).wait_recv())
    cur = rest_in[...].reshape(nx * REST, CELLS)
    prev = None
    weight = diag[rows : rows + nx * REST, :]
    for number in range(DEG):
        vh, vl = split2(cur)
        total = (
            dot(vh, plane[0])
            + dot(vl, plane[0])
            + dot(vh, plane[1])
            + dot(cross_ref[0], vh)
            + dot(cross_ref[0], vl)
            + dot(cross_ref[1], vh)
            + weight * cur
        )
        if prev is not None:
            total = 2.0 * total - prev
        prev, cur = cur, total
    rest_out[...] = cur.reshape(n, SLAB * REST, CELLS)
    peers(lambda d: ob_copy(d, me).start())
    rest_back[me] = rest_out[me]

    peers(lambda s: oa_copy(s, s).wait_recv())
    peers(lambda s: ob_copy(s, s).wait_recv())
    for p in range(SLAB):
        for d in range(n):
            out_ref[p, first_rest + REST * d : first_rest + REST * d + REST, :] = rest_back[
                d, REST * p : REST * p + REST, :
            ]
    for p in range(SLAB):
        x_copy(p).wait_send()

    def drain(d):
        pot_copy(d, me).wait_send()
        a_whole(d, me).wait_send()
        b_copy(d, me).wait_send()
        oa_copy(d, me).wait_send()
        ob_copy(d, me).wait_send()

    peers(drain)


def local_whole(orbitals, potential, rotation):
    n = lax.axis_size("space")
    band = lax.axis_index("band")
    held = orbitals.shape[0]
    nx = SLAB * n
    rows = nx * MAIN
    columns = lax.dynamic_slice_in_dim(rotation, band * held, held, axis=1)
    own = lax.dynamic_slice_in_dim(columns, band * held, held, axis=0)
    oth = lax.dynamic_slice_in_dim(columns, (1 - band) * held, held, axis=0)
    turn = jnp.stack([own.T, oth.T])
    f32, bf16 = jnp.float32, jnp.bfloat16
    vmem = pl.BlockSpec(memory_space=pltpu.VMEM)
    tile = (n, SLAB * REST, CELLS)
    sems = pltpu.SemaphoreType.DMA((n,))
    result = pl.pallas_call(
        functools.partial(kernel, n),
        out_shape=jax.ShapeDtypeStruct((SLAB, held, CELLS), f32),
        in_specs=[vmem, vmem, vmem, pl.BlockSpec(memory_space=pl.ANY), vmem, vmem],
        out_specs=vmem,
        scratch_shapes=[
            pltpu.VMEM((SLAB, held, CELLS), f32),
            pltpu.VMEM((SLAB, held, CELLS), f32),
            pltpu.VMEM((nx + 8, MAIN, CELLS), f32),
            pltpu.VMEM((nx + 8, MAIN, CELLS), f32),
            pltpu.VMEM((nx + 8, MAIN, CELLS), f32),
            pltpu.VMEM(tile, f32),
            pltpu.VMEM(tile, f32),
            pltpu.VMEM(tile, f32),
            pltpu.VMEM(tile, f32),
            pltpu.VMEM((n, 2 * SLAB, CELLS // 2), f32),
            pltpu.VMEM((nx * (MAIN + REST), CELLS), f32),
            pltpu.VMEM((2, CELLS, CELLS), bf16),
            pltpu.VMEM((rows, CELLS), f32),
            pltpu.VMEM((rows, CELLS), bf16),
            pltpu.VMEM((rows, CELLS), bf16),
            pltpu.SemaphoreType.DMA((SLAB,)),
            pltpu.SemaphoreType.DMA((SLAB,)),
            sems, sems, sems, sems, sems, sems, sems, sems, sems, sems,
            pltpu.SemaphoreType.DMA,
        ],
        compiler_params=pltpu.CompilerParams(
            collective_id=0, has_side_effects=True, vmem_limit_bytes=40 * 1024 * 1024
        ),
    )(
        jnp.transpose(orbitals, (1, 0, 2)),
        turn,
        potential.reshape(2 * SLAB, CELLS // 2),
        jnp.asarray(in_plane()),
        jnp.asarray(across_planes(nx)),
        jnp.asarray(spread(nx)),
    )
    return jnp.transpose(result, (1, 0, 2))


def local(orbitals, potential, rotation):
    n = lax.axis_size("space")
    fits = (
        lax.axis_size("band") == 2
        and n > 1
        and orbitals.shape == ((MAIN + REST) * n, SLAB, CELLS)
    )
    if fits:
        return local_whole(orbitals, potential, rotation)
    return local_halo(orbitals, potential, rotation)


def solution(mesh):
    placed = (P("band", "space", None), P("space", None), P())
    return jax.shard_map(
        local, mesh=mesh, in_specs=placed, out_specs=P("band", "space", None), check_vma=False
    )
```

```python
import functools

import jax
import jax.numpy as jnp
import numpy as np
from jax import lax
from jax.experimental import pallas as pl
from jax.experimental.pallas import tpu as pltpu
from jax.sharding import PartitionSpec as P

DEG = 4
NY = 16
NZ = 32
MESH = pl.DeviceIdType.MESH


coef_lap = (-205.0 / 72.0, 8.0 / 5.0, -1.0 / 5.0, 8.0 / 315.0, -1.0 / 560.0)
center_val = 6.0
half_width = 4.0

MAIN = 8
HALF = 4
REST = 2
SLAB = 4
CELLS = NY * NZ
WEIGHT = [-0.5 * c / half_width for c in coef_lap]
SHIFT = -1.5 * coef_lap[0] - center_val


def with_halo(block, sides, width):
    for axis, dim in sides:
        count = lax.axis_size(axis)
        forward = [(i, i + 1) for i in range(count - 1)]
        forward.append((count - 1, 0))
        backward = [(target, source) for source, target in forward]
        low = lax.ppermute(
            lax.slice_in_dim(block, block.shape[dim] - width, None, axis=dim), axis, forward
        )
        high = lax.ppermute(lax.slice_in_dim(block, 0, width, axis=dim), axis, backward)
        block = jnp.concatenate([low, block, high], axis=dim)
    return block


def cross_terms(field):
    nblk, planes, cells = field.shape
    cube = field.reshape(nblk, planes, NY, NZ)
    inner = jnp.zeros_like(cube)
    for shift_k in range(1, 5):
        inner = inner + coef_lap[shift_k] * (
            jnp.roll(cube, shift_k, 2)
            + jnp.roll(cube, -shift_k, 2)
            + jnp.roll(cube, shift_k, 3)
            + jnp.roll(cube, -shift_k, 3)
        )
    return inner.reshape(nblk, planes, cells)


def hamil_slab(field, potential):
    planes = field.shape[1]
    padded = with_halo(field, (("space", 1),), 4)
    lap = 3.0 * coef_lap[0] * field
    for shift_k in range(1, 5):
        upper = padded[:, 4 + shift_k : 4 + shift_k + planes]
        lower = padded[:, 4 - shift_k : 4 - shift_k + planes]
        lap = lap + coef_lap[shift_k] * (upper + lower)
    lap = lap + cross_terms(field)
    return -0.5 * lap + potential[None] * field


def chebyshev(start_y, potential, apply_h):
    prev_y = start_y
    curr_y = (apply_h(start_y, potential) - center_val * start_y) / half_width
    for step in range(1, DEG):
        next_y = 2.0 * (apply_h(curr_y, potential) - center_val * curr_y) / half_width - prev_y
        prev_y = curr_y
        curr_y = next_y
    return curr_y


def local_halo(orbitals, potential, rotation):
    curr_y = chebyshev(orbitals, potential, hamil_slab)
    turned = lax.dot_general(
        rotation,
        lax.all_to_all(curr_y, "band", split_axis=2, concat_axis=0, tiled=True),
        (((0,), (0,)), ((), ())),
        precision=lax.Precision.HIGHEST,
        preferred_element_type=jnp.float32,
    )
    return lax.all_to_all(turned, "band", split_axis=0, concat_axis=2, tiled=True)


def split_const(matrix):
    high = matrix.astype(np.float32).astype(jnp.bfloat16)
    low = (matrix - high.astype(np.float64)).astype(np.float32).astype(jnp.bfloat16)
    return np.stack([high, low])


def ring_matrix(size):
    ring = np.zeros((size, size))
    for at in range(size):
        for k in range(1, 5):
            ring[at, (at + k) % size] += WEIGHT[k]
            ring[at, (at - k) % size] += WEIGHT[k]
    return ring


def in_plane():
    return split_const(
        np.kron(ring_matrix(NY), np.eye(NZ)) + np.kron(np.eye(NY), ring_matrix(NZ))
    )


def spread(planes):
    rows = np.concatenate([np.repeat(np.arange(planes), m) for m in (HALF, REST)])
    picks = np.arange(2 * planes)
    return np.stack([rows[:, None] * 2 + half == picks[None] for half in range(2)]).astype(
        jnp.bfloat16
    )


def split2(value):
    high = value.astype(jnp.bfloat16)
    low = (value - high.astype(jnp.float32)).astype(jnp.bfloat16)
    return high, low


def dot(a, b):
    return jnp.dot(a, b, preferred_element_type=jnp.float32)


def kernel(
    n,
    y_ref,
    rt_ref,
    pot_ref,
    plane_hbm,
    spread_ref,
    out_ref,
    other,
    send,
    rest_send,
    bufs,
    rest_bufs,
    back,
    rest_back,
    pots,
    diag,
    plane,
    acc,
    high,
    low,
    x_send,
    x_recv,
    pot_send,
    pot_recv,
    in_send,
    in_recv,
    back_send,
    back_recv,
    plane_sem,
):
    me = lax.axis_index("space")
    band = lax.axis_index("band")
    nx = SLAB * n
    first_rest = MAIN * n
    sizes = (HALF, HALF, REST)
    work = [[bufs.at[c, i] for i in range(3)] for c in range(2)]
    work.append([rest_bufs.at[i] for i in range(3)])
    sends = [send.at[0], send.at[1], rest_send]
    backs = [back.at[0], back.at[1], rest_back]

    barrier = pltpu.get_barrier_semaphore()
    pl.semaphore_signal(
        barrier, inc=1, device_id={"band": 1 - band}, device_id_type=MESH
    )

    def peers(body):
        def step(k, carry):
            body(lax.rem(me + k, n))
            return carry

        lax.fori_loop(1, n, step, 0)

    peers(
        lambda d: pl.semaphore_signal(
            barrier, inc=1, device_id={"space": d}, device_id_type=MESH
        )
    )
    plane_copy = pltpu.make_async_copy(plane_hbm, plane, plane_sem)
    plane_copy.start()
    pl.semaphore_wait(barrier, n)

    units = [(pair, half) for pair in range(SLAB // 2) for half in range(2)]

    def lanes_of(half):
        return slice(half * (CELLS // 2), (half + 1) * (CELLS // 2))

    def x_copy(u):
        pair, half = units[u]
        at = (slice(2 * pair, 2 * pair + 2), slice(None), lanes_of(half))
        return pltpu.make_async_remote_copy(
            src_ref=y_ref.at[at],
            dst_ref=other.at[at],
            send_sem=x_send.at[u],
            recv_sem=x_recv.at[u],
            device_id={"band": 1 - band},
            device_id_type=MESH,
        )

    def space_copy(src, dst, send_sem, recv_sem, target):
        return pltpu.make_async_remote_copy(
            src_ref=src,
            dst_ref=dst,
            send_sem=send_sem,
            recv_sem=recv_sem,
            device_id={"space": target},
            device_id_type=MESH,
        )

    def slab_rows(c, s):
        tall = SLAB * sizes[c]
        return pl.ds(pl.multiple_of(tall * s + tall, 8), tall)

    def pot_copy(d, at):
        return space_copy(pot_ref, pots.at[at], pot_send.at[d], pot_recv.at[at], d)

    def part_copy(c, u, d, at):
        pair, half = units[u]
        tall = SLAB * sizes[c]
        rows = pl.ds(pl.multiple_of(tall * at + tall + 8 * pair, 8), 8)
        return space_copy(
            sends[c].at[d, 8 * pair : 8 * pair + 8, lanes_of(half)],
            work[c][0].at[rows, lanes_of(half)],
            in_send.at[c, d],
            in_recv.at[c, at],
            d,
        )

    def in_copy(c, d, at):
        return space_copy(
            sends[c].at[d], work[c][0].at[slab_rows(c, at)], in_send.at[c, d], in_recv.at[c, at], d
        )

    def back_copy(c, d, at):
        return space_copy(
            work[c][1].at[slab_rows(c, d)], backs[c].at[at], back_send.at[c, d], back_recv.at[c, at], d
        )

    for u in range(len(units)):
        x_copy(u).start()
    peers(lambda d: pot_copy(d, me).start())
    pots[me] = pot_ref[...]

    own_high, own_low = split2(rt_ref[0])
    oth_high, oth_low = split2(rt_ref[1])
    for u, (pair, half) in enumerate(units):
        lanes = lanes_of(half)
        turned = []
        for p in (2 * pair, 2 * pair + 1):
            vh, vl = split2(y_ref[p, :, lanes])
            turned.append(dot(own_high, vh) + dot(own_high, vl) + dot(own_low, vh))
        x_copy(u).wait_recv()
        for i in range(2):
            vh, vl = split2(other[2 * pair + i, :, lanes])
            turned[i] += dot(oth_high, vh) + dot(oth_high, vl) + dot(oth_low, vh)
        one, two = [t[:first_rest].reshape(n, MAIN, CELLS // 2) for t in turned]
        for c in range(2):
            part = slice(HALF * c, HALF * c + HALF)
            send[c, :, 8 * pair : 8 * pair + 8, lanes] = jnp.concatenate(
                [one[:, part], two[:, part]], axis=1
            )
            peers(lambda d, c=c, u=u: part_copy(c, u, d, me).start())
        for i in range(2):
            p = 2 * pair + i
            for d in range(n):
                rest_send[d, REST * p : REST * p + REST, lanes] = turned[i][
                    first_rest + REST * d : first_rest + REST * d + REST
                ]
    peers(lambda d: in_copy(2, d, me).start())
    for c in range(3):
        work[c][0][slab_rows(c, me), :] = sends[c][me]

    peers(lambda s: pot_copy(s, s).wait_recv())
    field = pots[...].reshape(2 * nx, CELLS // 2)
    fh = field.astype(jnp.bfloat16)
    fm, fl = split2(field - fh.astype(jnp.float32))
    for half in range(2):
        pick = spread_ref[half]
        diag[:, lanes_of(half)] = (dot(pick, fh) + dot(pick, fm) + dot(pick, fl) + SHIFT) * (
            1.0 / half_width
        )

    plane_copy.wait()

    def filter_chunk(c):
        m = sizes[c]
        rows, edge = nx * m, 4 * m
        weight_at = 0 if m == HALF else nx * HALF
        y0, y1, y2 = work[c]

        def wrap(ref):
            ref[0:edge, :] = ref[rows : rows + edge, :]
            ref[rows + edge : rows + 2 * edge, :] = ref[edge : 2 * edge, :]

        def put_split(g, lanes, value):
            hi, lo = split2(value)
            at = pl.ds(pl.multiple_of(g * 64, 64), 64)
            high[at, lanes] = hi
            low[at, lanes] = lo

        def each_group(body):
            def step(g, carry):
                for lane in range(CELLS // 128):
                    body(g, slice(128 * lane, 128 * lane + 128))
                return carry

            lax.fori_loop(0, rows // 64, step, 0)

        wrap(y0)
        each_group(
            lambda g, lanes: put_split(
                g, lanes, y0[pl.ds(pl.multiple_of(g * 64 + edge, 8), 64), lanes]
            )
        )
        order = [(y0, None, y1), (y1, y0, y2), (y2, y1, y0), (y0, y2, y1)]
        for number, (cur, prev, new) in enumerate(order):
            last = number == DEG - 1
            at = slice(0, rows)
            acc[at, :] = (
                dot(high[at, :], plane[0]) + dot(low[at, :], plane[0]) + dot(high[at, :], plane[1])
            )

            def update(g, lanes, cur=cur, prev=prev, new=new, last=last):
                wide = cur[pl.ds(pl.multiple_of(g * 64, 64), 64 + 2 * edge), lanes]
                mine = pl.ds(pl.multiple_of(g * 64 + edge, 8), 64)
                total = acc[pl.ds(pl.multiple_of(g * 64, 64), 64), lanes]
                weight = diag[pl.ds(pl.multiple_of(g * 64 + weight_at, 64), 64), lanes]
                total = total + weight * wide[edge : edge + 64]
                for k in range(1, 5):
                    up, down = edge + m * k, edge - m * k
                    total = total + WEIGHT[k] * (wide[up : up + 64] + wide[down : down + 64])
                if prev is not None:
                    total = 2.0 * total - prev[mine, lanes]
                new[mine, lanes] = total
                if not last:
                    put_split(g, lanes, total)

            each_group(update)
            if not last:
                wrap(new)

    for c in range(3):
        peers(lambda s, c=c: in_copy(c, s, s).wait_recv())
        filter_chunk(c)
        peers(lambda d, c=c: back_copy(c, d, me).start())
        backs[c][me] = work[c][1][slab_rows(c, me), :]

    for c in range(2):
        peers(lambda s, c=c: back_copy(c, s, s).wait_recv())
    for pair in range(SLAB // 2):
        for i in range(2):
            part = slice(8 * pair + HALF * i, 8 * pair + HALF * i + HALF)
            out_ref[2 * pair + i, 0:first_rest, :] = jnp.concatenate(
                [back[0, :, part, :], back[1, :, part, :]], axis=1
            ).reshape(first_rest, CELLS)
    peers(lambda s: back_copy(2, s, s).wait_recv())
    for p in range(SLAB):
        for d in range(n):
            out_ref[p, first_rest + REST * d : first_rest + REST * d + REST, :] = rest_back[
                d, REST * p : REST * p + REST, :
            ]
    for u in range(len(units)):
        x_copy(u).wait_send()

    def drain(d):
        pot_copy(d, me).wait_send()
        for c in range(3):
            in_copy(c, d, me).wait_send()
            back_copy(c, d, me).wait_send()

    peers(drain)


def local_whole(orbitals, potential, rotation):
    n = lax.axis_size("space")
    band = lax.axis_index("band")
    held = orbitals.shape[0]
    nx = SLAB * n
    columns = lax.dynamic_slice_in_dim(rotation, band * held, held, axis=1)
    own = lax.dynamic_slice_in_dim(columns, band * held, held, axis=0)
    oth = lax.dynamic_slice_in_dim(columns, (1 - band) * held, held, axis=0)
    turn = jnp.stack([own.T, oth.T])
    f32, bf16 = jnp.float32, jnp.bfloat16
    vmem = pl.BlockSpec(memory_space=pltpu.VMEM)
    half_tile, rest_tile = (n, SLAB * HALF, CELLS), (n, SLAB * REST, CELLS)
    sems, three = pltpu.SemaphoreType.DMA((n,)), pltpu.SemaphoreType.DMA((3, n))
    result = pl.pallas_call(
        functools.partial(kernel, n),
        out_shape=jax.ShapeDtypeStruct((SLAB, held, CELLS), f32),
        in_specs=[vmem, vmem, vmem, pl.BlockSpec(memory_space=pl.ANY), vmem],
        out_specs=vmem,
        scratch_shapes=[
            pltpu.VMEM((SLAB, held, CELLS), f32),
            pltpu.VMEM((2, *half_tile), f32),
            pltpu.VMEM(rest_tile, f32),
            pltpu.VMEM((2, 3, (nx + 8) * HALF, CELLS), f32),
            pltpu.VMEM((3, (nx + 8) * REST, CELLS), f32),
            pltpu.VMEM((2, *half_tile), f32),
            pltpu.VMEM(rest_tile, f32),
            pltpu.VMEM((n, 2 * SLAB, CELLS // 2), f32),
            pltpu.VMEM((nx * (HALF + REST), CELLS), f32),
            pltpu.VMEM((2, CELLS, CELLS), bf16),
            pltpu.VMEM((nx * HALF, CELLS), f32),
            pltpu.VMEM((nx * HALF, CELLS), bf16),
            pltpu.VMEM((nx * HALF, CELLS), bf16),
            pltpu.SemaphoreType.DMA((SLAB,)),
            pltpu.SemaphoreType.DMA((SLAB,)),
            sems, sems, three, three, three, three,
            pltpu.SemaphoreType.DMA,
        ],
        compiler_params=pltpu.CompilerParams(
            collective_id=0, has_side_effects=True, vmem_limit_bytes=40 * 1024 * 1024
        ),
    )(
        jnp.transpose(orbitals, (1, 0, 2)),
        turn,
        potential.reshape(2 * SLAB, CELLS // 2),
        jnp.asarray(in_plane()),
        jnp.asarray(spread(nx)),
    )
    return jnp.transpose(result, (1, 0, 2))


def local(orbitals, potential, rotation):
    n = lax.axis_size("space")
    fits = (
        lax.axis_size("band") == 2
        and n > 1
        and orbitals.shape == ((MAIN + REST) * n, SLAB, CELLS)
    )
    if fits:
        return local_whole(orbitals, potential, rotation)
    return local_halo(orbitals, potential, rotation)


def solution(mesh):
    placed = (P("band", "space", None), P("space", None), P())
    return jax.shard_map(
        local, mesh=mesh, in_specs=placed, out_specs=P("band", "space", None), check_vma=False
    )
```

```python
import functools

import jax
import jax.numpy as jnp
import numpy as np
from jax import lax
from jax.experimental import pallas as pl
from jax.experimental.pallas import tpu as pltpu
from jax.sharding import PartitionSpec as P

DEG = 4
NY = 16
NZ = 32
MESH = pl.DeviceIdType.MESH


coef_lap = (-205.0 / 72.0, 8.0 / 5.0, -1.0 / 5.0, 8.0 / 315.0, -1.0 / 560.0)
center_val = 6.0
half_width = 4.0

MAIN = 8
HALF = 4
REST = 2
SLAB = 4
CELLS = NY * NZ
WEIGHT = [-0.5 * c / half_width for c in coef_lap]
SHIFT = -1.5 * coef_lap[0] - center_val


def with_halo(block, sides, width):
    for axis, dim in sides:
        count = lax.axis_size(axis)
        forward = [(i, i + 1) for i in range(count - 1)]
        forward.append((count - 1, 0))
        backward = [(target, source) for source, target in forward]
        low = lax.ppermute(
            lax.slice_in_dim(block, block.shape[dim] - width, None, axis=dim), axis, forward
        )
        high = lax.ppermute(lax.slice_in_dim(block, 0, width, axis=dim), axis, backward)
        block = jnp.concatenate([low, block, high], axis=dim)
    return block


def cross_terms(field):
    nblk, planes, cells = field.shape
    cube = field.reshape(nblk, planes, NY, NZ)
    inner = jnp.zeros_like(cube)
    for shift_k in range(1, 5):
        inner = inner + coef_lap[shift_k] * (
            jnp.roll(cube, shift_k, 2)
            + jnp.roll(cube, -shift_k, 2)
            + jnp.roll(cube, shift_k, 3)
            + jnp.roll(cube, -shift_k, 3)
        )
    return inner.reshape(nblk, planes, cells)


def hamil_slab(field, potential):
    planes = field.shape[1]
    padded = with_halo(field, (("space", 1),), 4)
    lap = 3.0 * coef_lap[0] * field
    for shift_k in range(1, 5):
        upper = padded[:, 4 + shift_k : 4 + shift_k + planes]
        lower = padded[:, 4 - shift_k : 4 - shift_k + planes]
        lap = lap + coef_lap[shift_k] * (upper + lower)
    lap = lap + cross_terms(field)
    return -0.5 * lap + potential[None] * field


def chebyshev(start_y, potential, apply_h):
    prev_y = start_y
    curr_y = (apply_h(start_y, potential) - center_val * start_y) / half_width
    for step in range(1, DEG):
        next_y = 2.0 * (apply_h(curr_y, potential) - center_val * curr_y) / half_width - prev_y
        prev_y = curr_y
        curr_y = next_y
    return curr_y


def local_halo(orbitals, potential, rotation):
    curr_y = chebyshev(orbitals, potential, hamil_slab)
    turned = lax.dot_general(
        rotation,
        lax.all_to_all(curr_y, "band", split_axis=2, concat_axis=0, tiled=True),
        (((0,), (0,)), ((), ())),
        precision=lax.Precision.HIGHEST,
        preferred_element_type=jnp.float32,
    )
    return lax.all_to_all(turned, "band", split_axis=0, concat_axis=2, tiled=True)


def split_const(matrix):
    high = matrix.astype(np.float32).astype(jnp.bfloat16)
    low = (matrix - high.astype(np.float64)).astype(np.float32).astype(jnp.bfloat16)
    return np.stack([high, low])


def ring_matrix(size):
    ring = np.zeros((size, size))
    for at in range(size):
        for k in range(1, 5):
            ring[at, (at + k) % size] += WEIGHT[k]
            ring[at, (at - k) % size] += WEIGHT[k]
    return ring


def in_plane():
    return split_const(
        np.kron(ring_matrix(NY), np.eye(NZ)) + np.kron(np.eye(NY), ring_matrix(NZ))
    )


def spread(planes):
    rows = np.concatenate([np.repeat(np.arange(planes), m) for m in (HALF, REST)])
    picks = np.arange(2 * planes)
    return np.stack([rows[:, None] * 2 + half == picks[None] for half in range(2)]).astype(
        jnp.bfloat16
    )


def split2(value):
    high = value.astype(jnp.bfloat16)
    low = (value - high.astype(jnp.float32)).astype(jnp.bfloat16)
    return high, low


def dot(a, b):
    return jnp.dot(a, b, preferred_element_type=jnp.float32)


def kernel(
    n,
    y_ref,
    rt_ref,
    pot_ref,
    plane_hbm,
    spread_ref,
    out_ref,
    other,
    send,
    rest_send,
    bufs,
    rest_bufs,
    back,
    rest_back,
    pots,
    diag,
    plane,
    acc,
    high,
    low,
    x_send,
    x_recv,
    pot_send,
    pot_recv,
    in_send,
    in_recv,
    back_send,
    back_recv,
    plane_sem,
):
    me = lax.axis_index("space")
    band = lax.axis_index("band")
    nx = SLAB * n
    first_rest = MAIN * n
    sizes = (HALF, HALF, REST)
    work = [[bufs.at[c, i] for i in range(3)] for c in range(2)]
    work.append([rest_bufs.at[i] for i in range(3)])
    sends = [send.at[0], send.at[1], rest_send]
    backs = [back.at[0], back.at[1], rest_back]

    barrier = pltpu.get_barrier_semaphore()
    pl.semaphore_signal(
        barrier, inc=1, device_id={"band": 1 - band}, device_id_type=MESH
    )

    paired = n & (n - 1) == 0

    def partner(t):
        if not paired:
            return lax.rem(me + t + 1, n)
        k = n // 2 + (1 - 2 * (t % 2)) * ((t + 1) // 2)
        bits = [1 << b for b in range(n.bit_length() - 1)]
        return sum(((me // b + k // b) % 2) * b for b in bits)

    def peers(body):
        def step(t, carry):
            body(partner(t))
            return carry

        lax.fori_loop(0, n - 1, step, 0)

    peers(
        lambda d: pl.semaphore_signal(
            barrier, inc=1, device_id={"space": d}, device_id_type=MESH
        )
    )
    plane_copy = pltpu.make_async_copy(plane_hbm, plane, plane_sem)
    plane_copy.start()
    pl.semaphore_wait(barrier, n)

    units = [(pair, half) for pair in range(SLAB // 2) for half in range(2)]

    def lanes_of(half):
        return slice(half * (CELLS // 2), (half + 1) * (CELLS // 2))

    def x_copy(u):
        pair, half = units[u]
        at = (slice(2 * pair, 2 * pair + 2), slice(None), lanes_of(half))
        return pltpu.make_async_remote_copy(
            src_ref=y_ref.at[at],
            dst_ref=other.at[at],
            send_sem=x_send.at[u],
            recv_sem=x_recv.at[u],
            device_id={"band": 1 - band},
            device_id_type=MESH,
        )

    def space_copy(src, dst, send_sem, recv_sem, target):
        return pltpu.make_async_remote_copy(
            src_ref=src,
            dst_ref=dst,
            send_sem=send_sem,
            recv_sem=recv_sem,
            device_id={"space": target},
            device_id_type=MESH,
        )

    def slab_rows(c, s):
        tall = SLAB * sizes[c]
        return pl.ds(pl.multiple_of(tall * s + tall, 8), tall)

    def pot_copy(d, at):
        return space_copy(pot_ref, pots.at[at], pot_send.at[d], pot_recv.at[at], d)

    def part_copy(c, u, d, at):
        pair, half = units[u]
        tall = SLAB * sizes[c]
        rows = pl.ds(pl.multiple_of(tall * at + tall + 8 * pair, 8), 8)
        return space_copy(
            sends[c].at[d, 8 * pair : 8 * pair + 8, lanes_of(half)],
            work[c][0].at[rows, lanes_of(half)],
            in_send.at[c, d],
            in_recv.at[c, at],
            d,
        )

    def in_copy(c, d, at):
        return space_copy(
            sends[c].at[d], work[c][0].at[slab_rows(c, at)], in_send.at[c, d], in_recv.at[c, at], d
        )

    def back_copy(c, d, at):
        return space_copy(
            work[c][1].at[slab_rows(c, d)], backs[c].at[at], back_send.at[c, d], back_recv.at[c, at], d
        )

    for u in range(len(units)):
        x_copy(u).start()
    peers(lambda d: pot_copy(d, me).start())
    pots[me] = pot_ref[...]

    own_high, own_low = split2(rt_ref[0])
    oth_high, oth_low = split2(rt_ref[1])
    for u, (pair, half) in enumerate(units):
        lanes = lanes_of(half)
        turned = []
        for p in (2 * pair, 2 * pair + 1):
            vh, vl = split2(y_ref[p, :, lanes])
            turned.append(dot(own_high, vh) + dot(own_high, vl) + dot(own_low, vh))
        x_copy(u).wait_recv()
        for i in range(2):
            vh, vl = split2(other[2 * pair + i, :, lanes])
            turned[i] += dot(oth_high, vh) + dot(oth_high, vl) + dot(oth_low, vh)
        one, two = [t[:first_rest].reshape(n, MAIN, CELLS // 2) for t in turned]
        for c in range(2):
            part = slice(HALF * c, HALF * c + HALF)
            send[c, :, 8 * pair : 8 * pair + 8, lanes] = jnp.concatenate(
                [one[:, part], two[:, part]], axis=1
            )
            peers(lambda d, c=c, u=u: part_copy(c, u, d, me).start())
        for i in range(2):
            p = 2 * pair + i
            for d in range(n):
                rest_send[d, REST * p : REST * p + REST, lanes] = turned[i][
                    first_rest + REST * d : first_rest + REST * d + REST
                ]
    peers(lambda d: in_copy(2, d, me).start())
    for c in range(3):
        work[c][0][slab_rows(c, me), :] = sends[c][me]

    peers(lambda s: pot_copy(s, s).wait_recv())
    field = pots[...].reshape(2 * nx, CELLS // 2)
    fh = field.astype(jnp.bfloat16)
    fm, fl = split2(field - fh.astype(jnp.float32))
    for half in range(2):
        pick = spread_ref[half]
        diag[:, lanes_of(half)] = (dot(pick, fh) + dot(pick, fm) + dot(pick, fl) + SHIFT) * (
            1.0 / half_width
        )

    plane_copy.wait()

    def filter_chunk(c):
        m = sizes[c]
        rows, edge = nx * m, 4 * m
        weight_at = 0 if m == HALF else nx * HALF
        y0, y1, y2 = work[c]

        def wrap(ref):
            ref[0:edge, :] = ref[rows : rows + edge, :]
            ref[rows + edge : rows + 2 * edge, :] = ref[edge : 2 * edge, :]

        def put_split(g, lanes, value):
            hi, lo = split2(value)
            at = pl.ds(pl.multiple_of(g * 64, 64), 64)
            high[at, lanes] = hi
            low[at, lanes] = lo

        def each_group(body):
            def step(g, carry):
                for lane in range(CELLS // 128):
                    body(g, slice(128 * lane, 128 * lane + 128))
                return carry

            lax.fori_loop(0, rows // 64, step, 0)

        wrap(y0)
        each_group(
            lambda g, lanes: put_split(
                g, lanes, y0[pl.ds(pl.multiple_of(g * 64 + edge, 8), 64), lanes]
            )
        )
        order = [(y0, None, y1), (y1, y0, y2), (y2, y1, y0), (y0, y2, y1)]
        for number, (cur, prev, new) in enumerate(order):
            last = number == DEG - 1
            at = slice(0, rows)
            acc[at, :] = (
                dot(high[at, :], plane[0]) + dot(low[at, :], plane[0]) + dot(high[at, :], plane[1])
            )

            def update(g, lanes, cur=cur, prev=prev, new=new, last=last):
                wide = cur[pl.ds(pl.multiple_of(g * 64, 64), 64 + 2 * edge), lanes]
                mine = pl.ds(pl.multiple_of(g * 64 + edge, 8), 64)
                total = acc[pl.ds(pl.multiple_of(g * 64, 64), 64), lanes]
                weight = diag[pl.ds(pl.multiple_of(g * 64 + weight_at, 64), 64), lanes]
                total = total + weight * wide[edge : edge + 64]
                for k in range(1, 5):
                    up, down = edge + m * k, edge - m * k
                    total = total + WEIGHT[k] * (wide[up : up + 64] + wide[down : down + 64])
                if prev is not None:
                    total = 2.0 * total - prev[mine, lanes]
                new[mine, lanes] = total
                if not last:
                    put_split(g, lanes, total)

            each_group(update)
            if not last:
                wrap(new)

    for c in range(3):
        peers(lambda s, c=c: in_copy(c, s, s).wait_recv())
        filter_chunk(c)
        peers(lambda d, c=c: back_copy(c, d, me).start())
        backs[c][me] = work[c][1][slab_rows(c, me), :]

    for c in range(2):
        peers(lambda s, c=c: back_copy(c, s, s).wait_recv())
    for pair in range(SLAB // 2):
        for i in range(2):
            part = slice(8 * pair + HALF * i, 8 * pair + HALF * i + HALF)
            out_ref[2 * pair + i, 0:first_rest, :] = jnp.concatenate(
                [back[0, :, part, :], back[1, :, part, :]], axis=1
            ).reshape(first_rest, CELLS)
    peers(lambda s: back_copy(2, s, s).wait_recv())
    for p in range(SLAB):
        for d in range(n):
            out_ref[p, first_rest + REST * d : first_rest + REST * d + REST, :] = rest_back[
                d, REST * p : REST * p + REST, :
            ]
    for u in range(len(units)):
        x_copy(u).wait_send()

    def drain(d):
        pot_copy(d, me).wait_send()
        for c in range(3):
            in_copy(c, d, me).wait_send()
            back_copy(c, d, me).wait_send()

    peers(drain)


def local_whole(orbitals, potential, rotation):
    n = lax.axis_size("space")
    band = lax.axis_index("band")
    held = orbitals.shape[0]
    nx = SLAB * n
    columns = lax.dynamic_slice_in_dim(rotation, band * held, held, axis=1)
    own = lax.dynamic_slice_in_dim(columns, band * held, held, axis=0)
    oth = lax.dynamic_slice_in_dim(columns, (1 - band) * held, held, axis=0)
    turn = jnp.stack([own.T, oth.T])
    f32, bf16 = jnp.float32, jnp.bfloat16
    vmem = pl.BlockSpec(memory_space=pltpu.VMEM)
    half_tile, rest_tile = (n, SLAB * HALF, CELLS), (n, SLAB * REST, CELLS)
    sems, three = pltpu.SemaphoreType.DMA((n,)), pltpu.SemaphoreType.DMA((3, n))
    result = pl.pallas_call(
        functools.partial(kernel, n),
        out_shape=jax.ShapeDtypeStruct((SLAB, held, CELLS), f32),
        in_specs=[vmem, vmem, vmem, pl.BlockSpec(memory_space=pl.ANY), vmem],
        out_specs=vmem,
        scratch_shapes=[
            pltpu.VMEM((SLAB, held, CELLS), f32),
            pltpu.VMEM((2, *half_tile), f32),
            pltpu.VMEM(rest_tile, f32),
            pltpu.VMEM((2, 3, (nx + 8) * HALF, CELLS), f32),
            pltpu.VMEM((3, (nx + 8) * REST, CELLS), f32),
            pltpu.VMEM((2, *half_tile), f32),
            pltpu.VMEM(rest_tile, f32),
            pltpu.VMEM((n, 2 * SLAB, CELLS // 2), f32),
            pltpu.VMEM((nx * (HALF + REST), CELLS), f32),
            pltpu.VMEM((2, CELLS, CELLS), bf16),
            pltpu.VMEM((nx * HALF, CELLS), f32),
            pltpu.VMEM((nx * HALF, CELLS), bf16),
            pltpu.VMEM((nx * HALF, CELLS), bf16),
            pltpu.SemaphoreType.DMA((SLAB,)),
            pltpu.SemaphoreType.DMA((SLAB,)),
            sems, sems, three, three, three, three,
            pltpu.SemaphoreType.DMA,
        ],
        compiler_params=pltpu.CompilerParams(
            collective_id=0, has_side_effects=True, vmem_limit_bytes=40 * 1024 * 1024
        ),
    )(
        jnp.transpose(orbitals, (1, 0, 2)),
        turn,
        potential.reshape(2 * SLAB, CELLS // 2),
        jnp.asarray(in_plane()),
        jnp.asarray(spread(nx)),
    )
    return jnp.transpose(result, (1, 0, 2))


def local(orbitals, potential, rotation):
    n = lax.axis_size("space")
    fits = (
        lax.axis_size("band") == 2
        and n > 1
        and orbitals.shape == ((MAIN + REST) * n, SLAB, CELLS)
    )
    if fits:
        return local_whole(orbitals, potential, rotation)
    return local_halo(orbitals, potential, rotation)


def solution(mesh):
    placed = (P("band", "space", None), P("space", None), P())
    return jax.shard_map(
        local, mesh=mesh, in_specs=placed, out_specs=P("band", "space", None), check_vma=False
    )
```
